256 devices in a mesh: seq: 128 (over y_lo, z, x, core), dp: 2 (over y_hi).
Axes of the slice: x: 4, y: 4 (y_hi: 2, y_lo: 2; y = y_hi * 2 + y_lo), z: 8, core: 2. Of those that a mesh axis runs over, the one named last changes fastest.
Arguments:
- activations: bfloat16 [2, 512, 512, 768], P('dp', 'seq'), may hold values from -6 to 6
- grad_output: bfloat16 [2, 512, 512, 768], P('dp', 'seq'), may hold values from -24 to 24
- outer_factor: bfloat16 [512, 512], replicated, may hold values from -0.25 to 0.25
- inner_factor: bfloat16 [512, 512], replicated, may hold values from -0.25 to 0.25
- twiddle: float32 [512, 512], P('seq'), may hold values from 0.5 to 2
Outputs:
- grad_input: bfloat16 [2, 512, 512, 768], P('dp', 'seq')
- grad_outer: float32 [512, 512], P('seq')
- grad_inner: float32 [512, 512], P('seq')
- grad_twiddle: float32 [512, 512], P('seq')
The draws below stay inside these ranges and needn't reach their ends.
All inputs are finite; a program needn't handle non-finite values.
Results may differ from the reference program's by a relative error of at most 0.0061.
Values may be sent and summed in bfloat16 or wider, within the bound.
A program may use at most 128 MiB of HBM per device.

```python
import jax
import jax.numpy as jnp
from jax import lax

N1 = 512
N2 = 512
C = 768
SEQS = 2


def raised(entries, own_key, source, target, blocks, factor):
    def block_of(dim):
        return (jnp.arange(entries.shape[dim]) // (entries.shape[dim] // blocks)).reshape((-1,) + (1,) * (entries.ndim - 1 - dim))

    one_side = jax.random.permutation(own_key, blocks)[block_of(target)]
    far = (block_of(target) + blocks // 2) % blocks
    return jnp.where((block_of(source) == one_side) | (block_of(source) == far), factor * entries, entries)


def block_levels(key, extent, split, low, high):
    factor_of, own = 1.0, jax.random.fold_in(key, 6)
    for position, parts in split:
        steps = jnp.exp(jax.random.uniform(jax.random.fold_in(own, position), (parts,), jnp.float32, low / len(split), high / len(split)))
        factor_of = factor_of * jnp.repeat(steps, extent[position] // parts).reshape([-1 if axis == position else 1 for axis in range(len(extent))])
    return factor_of


def gaussian(rng, extent, deviation, limit, pieces=(), dtype=jnp.bfloat16):
    result = jax.random.normal(rng, extent, jnp.float32) * deviation
    if len(pieces) > 0:
        result = block_levels(rng, extent, pieces, -0.22, 0.18) * result
    return jnp.clip(result, min=-limit, max=limit).astype(dtype)


def gaussian_with(own_key, dims, deviation, bound, split, heavy, dtype=jnp.bfloat16):
    values = deviation * jax.random.normal(own_key, dims, jnp.float32)
    if split:
        values = values * block_levels(own_key, dims, split, -0.22, 0.18)
    return jnp.clip(raised(values, jax.random.fold_in(own_key, 3), *heavy), -bound, bound).astype(dtype)


def setup_inputs(seed: int = 0) -> dict:
    seeds = jax.random.split(jax.random.key(seed), 6)
    activations = gaussian(seeds[0], (SEQS, N1, N2, C), 1.0, 6.0, ((0, 2), (1, 128)))
    grad_output = gaussian_with(seeds[1], (SEQS, N1, N2, C), 1.0, 24.0, ((0, 2), (1, 128)), (2, 1, 128, 5.5))
    outer_factor = gaussian(seeds[2], (N1, N1), N1 ** -0.5, 0.25)
    inner_factor = gaussian(seeds[3], (N2, N2), N2 ** -0.5, 0.25)
    twiddle = jnp.clip(0.5 + 1.5 * jax.random.uniform(seeds[4], (N1, N2), jnp.float32) ** block_levels(seeds[4], (N1, N2), ((0, 128),), -0.2, 0.2), 0.5, 2.0)
    return dict(activations=activations, grad_output=grad_output, outer_factor=outer_factor, inner_factor=inner_factor, twiddle=twiddle)


def block_grads(carry, pair):
    acts, grads_out, outer_factor, inner_factor, twiddle = pair
    acts_f = acts.astype(jnp.float32)
    grads_f = grads_out.astype(jnp.float32)
    outer_f = outer_factor.astype(jnp.float32)
    inner_f = inner_factor.astype(jnp.float32)
    inner = jnp.einsum('kj,ijc->ikc', inner_f, acts_f)
    scaled = (inner * twiddle[:, :, None]).astype(jnp.bfloat16)
    mixed = jnp.einsum('ab,bjc->ajc', outer_f, scaled.astype(jnp.float32)).astype(jnp.bfloat16)
    grad_mixed = (grads_f * acts_f).astype(jnp.bfloat16)
    grad_gate = grads_f * mixed.astype(jnp.float32)
    grad_scaled = jnp.einsum('ab,ajc->bjc', outer_f, grad_mixed.astype(jnp.float32)).astype(jnp.bfloat16)
    outer_term = jnp.einsum('ajc,bjc->ab', grad_mixed.astype(jnp.float32), scaled.astype(jnp.float32))
    twiddle_term = jnp.sum(grad_scaled.astype(jnp.float32) * inner, axis=2)
    grad_inner_act = (grad_scaled.astype(jnp.float32) * twiddle[:, :, None]).astype(jnp.bfloat16)
    inner_term = jnp.einsum('ikc,ijc->kj', grad_inner_act.astype(jnp.float32), acts_f)
    grad_input = (grad_gate + jnp.einsum('kj,ikc->ijc', inner_f, grad_inner_act.astype(jnp.float32))).astype(jnp.bfloat16)
    return (carry[0] + outer_term, carry[1] + inner_term, carry[2] + twiddle_term), grad_input


def reference(activations, grad_output, outer_factor, inner_factor, twiddle):
    block_width = min(C, 128)
    block_count = C // block_width

    def split_blocks(array):
        shaped = array.reshape(SEQS, N1, N2, block_count, block_width)
        return shaped.transpose(0, 3, 1, 2, 4).reshape(SEQS * block_count, N1, N2, block_width)

    def step(carry, pair):
        return block_grads(carry, (pair[0], pair[1], outer_factor, inner_factor, twiddle))

    start = (jnp.zeros((N1, N1), jnp.float32), jnp.zeros((N2, N2), jnp.float32), jnp.zeros((N1, N2), jnp.float32))
    totals, grad_blocks = lax.scan(step, start, (split_blocks(activations), split_blocks(grad_output)))
    grad_input = grad_blocks.reshape(SEQS, block_count, N1, N2, block_width).transpose(0, 2, 3, 1, 4).reshape(SEQS, N1, N2, C)
    return grad_input, totals[0], totals[1], totals[2]
```

```python
import functools

import jax
import jax.numpy as jnp
from jax import lax
from jax.experimental import pallas as pl
from jax.experimental.pallas import tpu as pltpu
from jax.sharding import PartitionSpec as P

NY, NZ, NX, NC = 2, 8, 4, 2
ROWS = 4
JL = 8
CHUNKS = 3
LANES = 128
WIDE = NC * LANES
MESH = pl.DeviceIdType.MESH
BF = jnp.bfloat16
F32 = jnp.float32


def kernel(
    acts_hbm, go_hbm, outer_hbm, inner_hbm, tw_hbm,
    gi_hbm, g_outer, g_inner, g_tw, zr, rzs,
    acts, go, o_mat, f_mat, o_t, f_t, tw_rows, tw_cols, tw_acc, inner,
    zs, pr, ps, rzr, t1, t2, gm, gia, terms, staged,
    rs_a, rs_bs, rs_b, rs_cs, rs_c, tw_send, tw_recv,
    load_sem, store_sem, z_send, z_recv, p_send, p_recv, b_send, b_recv, c_send, c_recv, t_send, t_recv,
):
    n = o_mat.shape[0]
    block = n // NZ
    seq = lax.axis_index("seq")
    dp = lax.axis_index("dp")
    y, z, x, core = seq // (NZ * NX * NC), (seq // (NX * NC)) % NZ, (seq // NC) % NX, seq % NC
    here = (y * NX + x) * NC + core
    plane = NY * NX * NC

    def seq_of(y_, z_, x_, c_):
        return ((y_ * NZ + z_) * NX + x_) * NC + c_

    def z_peer(d):
        z_ = (z + d) % NZ
        return z_, {"seq": seq_of(y, z_, x, core)}

    def plane_peer(d):
        at = (here + d) % plane
        y_, x_, c_ = at // (NX * NC), (at // NC) % NX, at % NC
        return y_, x_, c_, {"seq": seq_of(y_, z, x_, c_)}

    def remote(src, dst, send, recv, device):
        pltpu.make_async_remote_copy(
            src_ref=src, dst_ref=dst, send_sem=send, recv_sem=recv, device_id=device, device_id_type=MESH
        ).start()

    def local(src, dst, sem):
        pltpu.make_async_copy(src, dst, sem).start()

    def wait(ref, sem):
        pltpu.make_async_copy(ref, ref, sem).wait()

    def chunk_loads(k):
        lanes = pl.ds(k * WIDE, WIDE)
        return [
            pltpu.make_async_copy(acts_hbm.at[:, :, lanes], acts.at[:, :, lanes], load_sem.at[2 * k]),
            pltpu.make_async_copy(go_hbm.at[:, :, lanes], go.at[:, :, lanes], load_sem.at[2 * k + 1]),
        ]

    weight_loads = [
        pltpu.make_async_copy(inner_hbm, f_mat, load_sem.at[2 * CHUNKS]),
        pltpu.make_async_copy(tw_hbm, tw_rows, load_sem.at[2 * CHUNKS + 1]),
        pltpu.make_async_copy(outer_hbm, o_mat, load_sem.at[2 * CHUNKS + 2]),
    ]
    for k in range(CHUNKS):
        for copy in chunk_loads(k):
            copy.start()
    for copy in weight_loads:
        copy.start()

    barrier = pltpu.get_barrier_semaphore()

    @pl.loop(1, NZ)
    def _(d):
        pl.semaphore_signal(barrier, 1, device_id=z_peer(d)[1], device_id_type=MESH)

    @pl.loop(1, plane)
    def _(d):
        pl.semaphore_signal(barrier, 1, device_id=plane_peer(d)[3], device_id_type=MESH)

    for c_ in range(NC):
        pl.semaphore_signal(
            barrier, 1, device_id={"seq": seq_of(y, z, x, c_), "dp": 1 - dp}, device_id_type=MESH
        )

    def send_z(src, dst, unit):
        @pl.loop(1, NZ)
        def _(d):
            z_, device = z_peer(d)
            remote(src.at[z_], dst.at[z], z_send.at[unit], z_recv.at[unit], device)

        local(src.at[z], dst.at[z], z_recv.at[unit])

    def wait_z(dst, unit):
        wait(dst, z_recv.at[unit])

    def wait_z_sent(src, unit):
        wait(src.at[pl.ds(0, NZ - 1)], z_send.at[unit])

    def send_out(u):
        send_z(zs.at[u % CHUNKS], zr.at[u], u)

    def send_back(u):
        send_z(rzs.at[u], rzr.at[u], 2 * CHUNKS + u)

    def send_plane_out(u):
        @pl.loop(1, plane)
        def _(d):
            y_, x_, c_, device = plane_peer(d)
            remote(
                zr.at[u, :, y_ * NX + x_, c_], pr.at[u, y, :, x * NC + core], p_send.at[u], p_recv.at[u], device
            )

        local(zr.at[u, :, y * NX + x, core], pr.at[u, y, :, x * NC + core], p_recv.at[u])

    def send_plane_back(u):
        unit = 2 * CHUNKS + u
        slot = u % CHUNKS

        @pl.loop(1, plane)
        def _(d):
            y_, x_, c_, device = plane_peer(d)
            remote(
                ps.at[slot, y_, :, x_ * NC + c_], rzs.at[u, :, y * NX + x, core],
                p_send.at[unit], p_recv.at[unit], device,
            )

        local(ps.at[slot, y, :, x * NC + core], rzs.at[u, :, y * NX + x, core], p_recv.at[unit])

    def wait_plane_sent(unit):
        wait(t_blocks(), p_send.at[unit])

    def t_blocks():
        return pr.at[0].reshape(n // ROWS, ROWS * JL, LANES).at[pl.ds(0, (plane - 1) * NZ)]

    def pack(slot, value):
        @pl.loop(0, NZ)
        def _(z_):
            for h in range(NC):
                for pair in range(ROWS // 2):
                    halves = [
                        value(2 * pair + i, z_, h).reshape(block // JL, 1, JL, LANES) for i in range(2)
                    ]
                    both = jnp.concatenate(halves, axis=1).reshape(block // JL, 2 * JL, LANES)
                    zs[slot, z_, :, h, pl.ds(pair * 2 * JL, 2 * JL), :] = both.astype(BF)

    def make_gm(k):
        for copy in chunk_loads(k):
            copy.wait()

        def value(r, z_, h):
            rows, lanes = pl.ds(z_ * block, block), pl.ds(k * WIDE + h * LANES, LANES)
            return go[r, rows, lanes].astype(F32) * acts[r, rows, lanes].astype(F32)

        pack(k, value)

    def make_scaled(k):
        lanes = pl.ds(k * WIDE, WIDE)

        @pl.loop(0, ROWS)
        def _(r):
            inner[r, :, lanes] = jnp.dot(f_mat[...], acts[r, :, lanes], preferred_element_type=F32)

        def value(r, z_, h):
            rows = pl.ds(z_ * block, block)
            return inner[r, rows, pl.ds(k * WIDE + h * LANES, LANES)] * tw_cols[r, rows, :]

        pack(k, value)

    def prepare():
        for copy in weight_loads:
            copy.wait()
        f_t[...] = f_mat[...].astype(F32).T.astype(BF)
        o_t[...] = o_mat[...].astype(F32).T.astype(BF)
        for r in range(ROWS):
            tw_cols[r] = jnp.broadcast_to(tw_rows[r : r + 1, :], (LANES, n)).T
        tw_acc[...] = jnp.zeros_like(tw_acc)
        terms[...] = jnp.zeros_like(terms)

    def add_term(which, left, right):
        total = lax.dot_general(left, right, (((1,), (1,)), ((), ())), preferred_element_type=F32)
        for half in range(NC):
            part = total[:, half * (n // NC) : (half + 1) * (n // NC)]
            terms[which, half] += part.reshape(NY, NZ, NX, n // (NY * NZ * NX), n // NC)

    def mix(u):
        k, slot = u % CHUNKS, u % CHUNKS
        rows = NX * NC * ROWS * JL

        for y_ in range(NY):
            @pl.loop(0, NZ)
            def _(z_):
                at = pl.multiple_of((y_ * NZ + z_) * rows, rows)
                t1[pl.ds(at, rows), :] = pr[u, y_, z_].astype(F32).reshape(rows, LANES)

        for q in range(JL // 2):
            two = [t1[pl.ds(2 * q + i, n, stride=JL), :] for i in range(2)]
            piece = jnp.concatenate(two, axis=1).astype(BF)
            if u < CHUNKS:
                gm[k, q] = piece
                mixed = jnp.dot(o_t[...], piece, preferred_element_type=F32)
            else:
                mixed = jnp.dot(o_mat[...], piece, preferred_element_type=F32)
                add_term(0, gm[k, q], piece)
            for i in range(2):
                t2[pl.ds(2 * q + i, n, stride=JL), :] = mixed[:, i * LANES : (i + 1) * LANES]

        for y_ in range(NY):
            @pl.loop(0, NZ)
            def _(z_):
                at = pl.multiple_of((y_ * NZ + z_) * rows, rows)
                ps[slot, y_, z_] = t2[pl.ds(at, rows), :].reshape(NX * NC, ROWS * JL, LANES).astype(BF)

    def unpack(u, r, z_, h):
        tile = rzr[u, z_, :, h, pl.ds((r // 2) * 2 * JL, 2 * JL), :].astype(F32)
        return tile.reshape(block // JL, 2, JL, LANES)[:, r % 2].reshape(block, LANES)

    def finish_scaled(k):
        lanes = pl.ds(k * WIDE, WIDE)
        for r in range(ROWS):
            @pl.loop(0, NZ)
            def _(z_):
                rows = pl.ds(z_ * block, block)
                for h in range(NC):
                    gs = unpack(k, r, z_, h)
                    tw_acc[r, rows, :] += gs * inner[r, rows, pl.ds(k * WIDE + h * LANES, LANES)]
                    gia[rows, pl.ds(h * LANES, LANES)] = (gs * tw_cols[r, rows, :]).astype(BF)

            add_term(1, gia[...], acts[r, :, lanes])
            inner[r, :, lanes] = jnp.dot(f_t[...], gia[...], preferred_element_type=F32)

    def chunk_store(k):
        lanes = pl.ds(k * WIDE, WIDE)
        return pltpu.make_async_copy(staged.at[:, :, lanes], gi_hbm.at[:, :, lanes], store_sem.at[k])

    def finish_mixed(k):
        for r in range(ROWS):
            @pl.loop(0, NZ)
            def _(z_):
                rows = pl.ds(z_ * block, block)
                for h in range(NC):
                    lanes = pl.ds(k * WIDE + h * LANES, LANES)
                    gate = go[r, rows, lanes].astype(F32) * unpack(CHUNKS + k, r, z_, h)
                    staged[r, rows, lanes] = (gate + inner[r, rows, lanes]).astype(BF)

        chunk_store(k).start()

    def reduce_plane(which):
        unit = 4 * CHUNKS + which

        @pl.loop(1, plane)
        def _(d):
            y_, x_, c_, device = plane_peer(d)
            remote(
                terms.at[which, c_, y_, :, x_], rs_a.at[which, here], p_send.at[unit], p_recv.at[unit], device
            )

        local(terms.at[which, core, y, :, x], rs_a.at[which, here], p_recv.at[unit])

    def reduce_z(which):
        unit = 4 * CHUNKS + which
        wait(rs_a.at[which], p_recv.at[unit])
        total = rs_a[which, 0]
        for i in range(1, plane):
            total += rs_a[which, i]
        rs_bs[which] = total

        @pl.loop(1, NZ)
        def _(d):
            z_, device = z_peer(d)
            remote(rs_bs.at[which, z_], rs_b.at[which, z], b_send.at[which], b_recv.at[which], device)

        local(rs_bs.at[which, z], rs_b.at[which, z], b_recv.at[which])

    def reduce_last(which):
        wait(rs_b.at[which], b_recv.at[which])
        total = rs_b[which, 0]
        for i in range(1, NZ):
            total += rs_b[which, i]
        rs_cs[which] = total
        here_ = dp * NC + core

        @pl.loop(1, 2 * NC)
        def _(d):
            at = (here_ + d) % (2 * NC)
            device = {"seq": seq_of(y, z, x, at % NC), "dp": at // NC}
            remote(rs_cs.at[which], rs_c.at[which, here_], c_send.at[which], c_recv.at[which], device)

        local(rs_cs.at[which], rs_c.at[which, here_], c_recv.at[which])

    def reduced(which, out):
        wait(rs_c.at[which], c_recv.at[which])
        both = rs_c[which, :NC] + rs_c[which, NC:]
        full = jnp.concatenate([both[i] for i in range(NC)], axis=1)
        out[...] = jnp.where(core == 0, full[:ROWS], full[ROWS:])

    def send_twiddle():
        rows = [jnp.sum(tw_acc[r].T, axis=0, keepdims=True) for r in range(ROWS)]
        tw_send[...] = jnp.concatenate(rows + rows, axis=0)
        remote(tw_send, tw_recv, t_send.at[0], t_recv.at[0], {"seq": seq, "dp": 1 - dp})

    make_gm(0)
    pl.semaphore_wait(barrier, NZ - 1 + plane - 1 + NC)
    send_out(0)
    make_gm(1)
    send_out(1)
    make_gm(2)
    prepare()
    for tick in range(4 * CHUNKS):
        out = tick < 2 * CHUNKS
        if out:
            wait_z(zr.at[tick], tick)
        else:
            wait_z(rzr.at[tick - 2 * CHUNKS], tick)
        after = tick + 2
        if after < 2 * CHUNKS:
            send_out(after)
        elif after < 4 * CHUNKS:
            wait(rzs.at[after - 2 * CHUNKS], p_recv.at[after])
            send_back(after - 2 * CHUNKS)
        if out:
            send_plane_out(tick)
        if tick < CHUNKS:
            wait_z_sent(zs.at[tick % CHUNKS], tick)
            make_scaled(tick)
        if 1 <= tick <= 2 * CHUNKS:
            u = tick - 1
            wait(pr.at[u], p_recv.at[u])
            if u >= CHUNKS:
                wait_plane_sent(2 * CHUNKS + u - CHUNKS)
            mix(u)
            send_plane_back(u)
        if tick == 2 * CHUNKS:
            reduce_plane(0)
        if tick == 2 * CHUNKS + 1:
            reduce_z(0)
        if tick == 2 * CHUNKS + 2:
            reduce_last(0)
        if 2 * CHUNKS <= tick < 3 * CHUNKS:
            finish_scaled(tick - 2 * CHUNKS)
        if tick == 3 * CHUNKS - 1:
            reduce_plane(1)
            send_twiddle()
        if tick == 3 * CHUNKS:
            reduce_z(1)
            reduced(0, g_outer)
        if tick == 3 * CHUNKS + 1:
            reduce_last(1)
        if tick >= 3 * CHUNKS:
            finish_mixed(tick - 3 * CHUNKS)

    reduced(1, g_inner)
    wait(tw_recv, t_recv.at[0])
    g_tw[...] = tw_send[:ROWS] + tw_recv[:ROWS]

    for unit in range(CHUNKS, 2 * CHUNKS):
        wait_z_sent(zs.at[0], unit)
    for unit in range(2 * CHUNKS, 4 * CHUNKS):
        wait_z_sent(rzs.at[0], unit)
    for unit in range(4 * CHUNKS):
        if not 2 * CHUNKS <= unit < 3 * CHUNKS:
            wait_plane_sent(unit)
    for which in range(2):
        wait(rs_a.at[which, pl.ds(0, plane - 1)], p_send.at[4 * CHUNKS + which])
        wait(rs_b.at[which, pl.ds(0, NZ - 1)], b_send.at[which])
        wait(rs_c.at[which, pl.ds(0, 2 * NC - 1)], c_send.at[which])
    wait(tw_recv, t_send.at[0])
    for k in range(CHUNKS):
        chunk_store(k).wait()


def per_device(activations, grad_output, outer_factor, inner_factor, twiddle):
    acts, grads = activations[0], grad_output[0]
    rows, n, channels = acts.shape
    assert rows == ROWS and n == JL * NY * NZ * NX and channels == CHUNKS * WIDE
    plane, block = NY * NX * NC, ROWS * JL
    dma = pltpu.SemaphoreType.DMA
    vm = pltpu.VMEM
    units = 2 * CHUNKS
    rowed = (NZ, NY * NX, NC, block, LANES)
    columned = (NY, NZ, NX * NC, block, LANES)
    part = (n // (NY * NZ * NX), n // NC)
    small = jax.ShapeDtypeStruct((ROWS, n), F32)
    any_spec = pl.BlockSpec(memory_space=pl.ANY)
    vmem_spec = pl.BlockSpec(memory_space=pltpu.VMEM)
    slots = jax.ShapeDtypeStruct((units,) + rowed, BF)
    scratch = [
        vm((ROWS, n, channels), BF),
        vm((ROWS, n, channels), BF),
        vm((n, n), BF), vm((n, n), BF), vm((n, n), BF), vm((n, n), BF),
        vm((ROWS, n), F32),
        vm((ROWS, n, LANES), F32),
        vm((ROWS, n, LANES), F32),
        vm((ROWS, n, channels), F32),
        vm((CHUNKS,) + rowed, BF),
        vm((units,) + columned, BF),
        vm((CHUNKS,) + columned, BF),
        vm((units,) + rowed, BF),
        vm((n * JL, LANES), F32),
        vm((n * JL, LANES), F32),
        vm((CHUNKS, JL // 2, n, WIDE), BF),
        vm((n, WIDE), BF),
        vm((2, NC, NY, NZ, NX) + part, F32),
        vm((ROWS, n, channels), BF),
        vm((2, plane, NZ) + part, F32),
        vm((2, NZ) + part, F32),
        vm((2, NZ) + part, F32),
        vm((2,) + part, F32),
        vm((2, 2 * NC) + part, F32),
        vm((2 * ROWS, n), F32),
        vm((2 * ROWS, n), F32),
        dma((2 * CHUNKS + 3,)), dma((CHUNKS,)),
        dma((2 * units,)), dma((2 * units,)),
        dma((2 * units + 2,)), dma((2 * units + 2,)),
        dma((2,)), dma((2,)), dma((2,)), dma((2,)), dma((1,)), dma((1,)),
    ]
    outs = pl.pallas_call(
        kernel,
        out_shape=[jax.ShapeDtypeStruct(acts.shape, BF), small, small, small, slots, slots],
        in_specs=[any_spec] * 5,
        out_specs=[any_spec, vmem_spec, vmem_spec, vmem_spec, any_spec, any_spec],
        scratch_shapes=scratch,
        compiler_params=pltpu.CompilerParams(
            collective_id=0, has_side_effects=True, vmem_limit_bytes=60 * 2**20
        ),
        name="monarch_backward",
    )(acts, grads, outer_factor, inner_factor, twiddle)
    return outs[0][None], outs[1], outs[2], outs[3]


def solution(mesh):
    placed = (P("dp", "seq", None, None), P("dp", "seq", None, None), P(), P(), P("seq", None))
    return jax.shard_map(
        per_device,
        mesh=mesh,
        in_specs=placed,
        out_specs=(P("dp", "seq", None, None), P("seq", None), P("seq", None), P("seq", None)),
        check_vma=False,
    )
```

```python
import functools

import jax
import jax.numpy as jnp
from jax import lax
from jax.experimental import pallas as pl
from jax.experimental.pallas import tpu as pltpu
from jax.sharding import PartitionSpec as P

NY, NZ, NX, NC = 2, 8, 4, 2
ROWS = 4
JL = 8
CHUNKS = 3
LANES = 128
WIDE = NC * LANES
MESH = pl.DeviceIdType.MESH
BF = jnp.bfloat16
F32 = jnp.float32


def kernel(
    acts_hbm, go_hbm, outer_hbm, inner_hbm, tw_hbm,
    gi, g_outer, g_inner, g_tw, zr, rzs,
    acts, go, o_mat, f_mat, o_t, f_t, tw_rows, tw_cols, tw_acc, inner,
    zs, pr, ps, rzr, t1, t2, gm, gia, terms,
    rs_a, rs_bs, rs_b, rs_cs, rs_c, tw_send, tw_recv,
    load_sem, first_sem, last_recv, z_send, z_recv, p_send, p_recv, b_send, b_recv, c_send, c_recv, t_send, t_recv,
):
    n = o_mat.shape[0]
    block = n // NZ
    seq = lax.axis_index("seq")
    dp = lax.axis_index("dp")
    y, z, x, core = seq // (NZ * NX * NC), (seq // (NX * NC)) % NZ, (seq // NC) % NX, seq % NC
    here = (y * NX + x) * NC + core
    plane = NY * NX * NC

    def seq_of(y_, z_, x_, c_):
        return ((y_ * NZ + z_) * NX + x_) * NC + c_

    def z_peer(d):
        z_ = (z + d) % NZ
        return z_, {"seq": seq_of(y, z_, x, core)}

    def plane_peer(d):
        at = (here + d) % plane
        y_, x_, c_ = at // (NX * NC), (at // NC) % NX, at % NC
        return y_, x_, c_, {"seq": seq_of(y_, z, x_, c_)}

    def remote(src, dst, send, recv, device):
        pltpu.make_async_remote_copy(
            src_ref=src, dst_ref=dst, send_sem=send, recv_sem=recv, device_id=device, device_id_type=MESH
        ).start()

    def local(src, dst, sem):
        pltpu.make_async_copy(src, dst, sem).start()

    def wait(ref, sem):
        pltpu.make_async_copy(ref, ref, sem).wait()

    def chunk_loads(k):
        lanes = pl.ds(k * WIDE, WIDE)
        return [
            pltpu.make_async_copy(acts_hbm.at[:, :, lanes], acts.at[:, :, lanes], load_sem.at[2 * k]),
            pltpu.make_async_copy(go_hbm.at[:, :, lanes], go.at[:, :, lanes], load_sem.at[2 * k + 1]),
        ]

    weight_loads = [
        pltpu.make_async_copy(inner_hbm, f_mat, load_sem.at[2 * CHUNKS]),
        pltpu.make_async_copy(tw_hbm, tw_rows, load_sem.at[2 * CHUNKS + 1]),
        pltpu.make_async_copy(outer_hbm, o_mat, load_sem.at[2 * CHUNKS + 2]),
    ]

    def nth(i):
        return (z + NZ + (i // 2 + 1) * (1 - 2 * (i % 2))) % NZ

    def first_loads(z_):
        part = (slice(None), pl.ds(z_ * block, block), pl.ds(0, WIDE))
        return [
            pltpu.make_async_copy(acts_hbm.at[part], acts.at[part], first_sem.at[0, z_]),
            pltpu.make_async_copy(go_hbm.at[part], go.at[part], first_sem.at[1, z_]),
        ]

    for i in range(2):
        for copy in first_loads(nth(i)):
            copy.start()

    barrier = pltpu.get_barrier_semaphore()

    @pl.loop(1, NZ)
    def _(d):
        pl.semaphore_signal(barrier, 1, device_id=z_peer(d)[1], device_id_type=MESH)

    @pl.loop(1, plane)
    def _(d):
        pl.semaphore_signal(barrier, 1, device_id=plane_peer(d)[3], device_id_type=MESH)

    for c_ in range(NC):
        pl.semaphore_signal(
            barrier, 1, device_id={"seq": seq_of(y, z, x, c_), "dp": 1 - dp}, device_id_type=MESH
        )

    @pl.loop(2, NZ - 1)
    def _(i):
        for copy in first_loads(nth(i)):
            copy.start()

    for copy in first_loads(z):
        copy.start()
    for k in range(1, CHUNKS):
        for copy in chunk_loads(k):
            copy.start()
    for copy in weight_loads:
        copy.start()

    def send_z(src, dst, unit):
        @pl.loop(1, NZ)
        def _(d):
            z_, device = z_peer(d)
            remote(src.at[z_], dst.at[z], z_send.at[unit], z_recv.at[unit], device)

        local(src.at[z], dst.at[z], z_recv.at[unit])

    def wait_z(dst, unit):
        wait(dst, z_recv.at[unit])

    def wait_z_sent(src, unit):
        wait(src.at[pl.ds(0, NZ - 1)], z_send.at[unit])

    def send_out(u):
        send_z(zs.at[u % CHUNKS], zr.at[u], u)

    def send_back(u):
        send_z(rzs.at[u], rzr.at[u], 2 * CHUNKS + u)

    def send_last():
        u, unit = 2 * CHUNKS - 1, 4 * CHUNKS - 1

        @pl.loop(0, NZ - 1)
        def _(i):
            z_ = nth(i)
            device = {"seq": seq_of(y, z_, x, core)}
            remote(rzs.at[u, z_], rzr.at[u, z], z_send.at[unit], last_recv.at[z], device)

        local(rzs.at[u, z], rzr.at[u, z], last_recv.at[z])

    def send_plane_out(u):
        @pl.loop(1, plane)
        def _(d):
            y_, x_, c_, device = plane_peer(d)
            remote(
                zr.at[u, :, y_ * NX + x_, c_], pr.at[u, y, :, x * NC + core], p_send.at[u], p_recv.at[u], device
            )

        local(zr.at[u, :, y * NX + x, core], pr.at[u, y, :, x * NC + core], p_recv.at[u])

    def send_plane_back(u):
        unit = 2 * CHUNKS + u
        slot = u % CHUNKS

        @pl.loop(1, plane)
        def _(d):
            y_, x_, c_, device = plane_peer(d)
            remote(
                ps.at[slot, y_, :, x_ * NC + c_], rzs.at[u, :, y * NX + x, core],
                p_send.at[unit], p_recv.at[unit], device,
            )

        local(ps.at[slot, y, :, x * NC + core], rzs.at[u, :, y * NX + x, core], p_recv.at[unit])

    def wait_plane_sent(unit):
        wait(t_blocks(), p_send.at[unit])

    def t_blocks():
        return pr.at[0].reshape(n // ROWS, ROWS * JL, LANES).at[pl.ds(0, (plane - 1) * NZ)]

    def pack(slot, z_, value):
        for h in range(NC):
            for pair in range(ROWS // 2):
                halves = [value(2 * pair + i, z_, h).reshape(block // JL, 1, JL, LANES) for i in range(2)]
                both = jnp.concatenate(halves, axis=1).reshape(block // JL, 2 * JL, LANES)
                zs[slot, z_, :, h, pl.ds(pair * 2 * JL, 2 * JL), :] = both.astype(BF)

    def gm_value(k):
        def value(r, z_, h):
            rows, lanes = pl.ds(z_ * block, block), pl.ds(k * WIDE + h * LANES, LANES)
            return go[r, rows, lanes].astype(F32) * acts[r, rows, lanes].astype(F32)

        return value

    def make_gm(k):
        for copy in chunk_loads(k):
            copy.wait()

        @pl.loop(0, NZ)
        def _(z_):
            pack(k, z_, gm_value(k))

    def send_first():
        @pl.loop(0, NZ - 1)
        def _(i):
            z_ = nth(i)
            for copy in first_loads(z_):
                copy.wait()
            pack(0, z_, gm_value(0))
            remote(zs.at[0, z_], zr.at[0, z], z_send.at[0], z_recv.at[0], {"seq": seq_of(y, z_, x, core)})

        for copy in first_loads(z):
            copy.wait()
        pack(0, z, gm_value(0))
        local(zs.at[0, z], zr.at[0, z], z_recv.at[0])

    def make_scaled(k):
        lanes = pl.ds(k * WIDE, WIDE)

        @pl.loop(0, ROWS)
        def _(r):
            inner[r, :, lanes] = jnp.dot(f_mat[...], acts[r, :, lanes], preferred_element_type=F32)

        def value(r, z_, h):
            rows = pl.ds(z_ * block, block)
            return inner[r, rows, pl.ds(k * WIDE + h * LANES, LANES)] * tw_cols[r, rows, :]

        @pl.loop(0, NZ)
        def _(z_):
            pack(k, z_, value)

    def prepare():
        for copy in weight_loads:
            copy.wait()
        f_t[...] = f_mat[...].astype(F32).T.astype(BF)
        o_t[...] = o_mat[...].astype(F32).T.astype(BF)
        for r in range(ROWS):
            tw_cols[r] = jnp.broadcast_to(tw_rows[r : r + 1, :], (LANES, n)).T
        tw_acc[...] = jnp.zeros_like(tw_acc)
        terms[...] = jnp.zeros_like(terms)

    def add_term(which, left, right):
        total = lax.dot_general(left, right, (((1,), (1,)), ((), ())), preferred_element_type=F32)
        for half in range(NC):
            part = total[:, half * (n // NC) : (half + 1) * (n // NC)]
            terms[which, half] += part.reshape(NY, NZ, NX, n // (NY * NZ * NX), n // NC)

    def mix(u):
        k, slot = u % CHUNKS, u % CHUNKS
        rows = NX * NC * ROWS * JL

        for y_ in range(NY):
            @pl.loop(0, NZ)
            def _(z_):
                at = pl.multiple_of((y_ * NZ + z_) * rows, rows)
                t1[pl.ds(at, rows), :] = pr[u, y_, z_].astype(F32).reshape(rows, LANES)

        for q in range(JL // 2):
            two = [t1[pl.ds(2 * q + i, n, stride=JL), :] for i in range(2)]
            piece = jnp.concatenate(two, axis=1).astype(BF)
            if u < CHUNKS:
                gm[k, q] = piece
                mixed = jnp.dot(o_t[...], piece, preferred_element_type=F32)
            else:
                mixed = jnp.dot(o_mat[...], piece, preferred_element_type=F32)
                add_term(0, gm[k, q], piece)
            for i in range(2):
                t2[pl.ds(2 * q + i, n, stride=JL), :] = mixed[:, i * LANES : (i + 1) * LANES]

        for y_ in range(NY):
            @pl.loop(0, NZ)
            def _(z_):
                at = pl.multiple_of((y_ * NZ + z_) * rows, rows)
                ps[slot, y_, z_] = t2[pl.ds(at, rows), :].reshape(NX * NC, ROWS * JL, LANES).astype(BF)

    def unpack(u, r, z_, h):
        tile = rzr[u, z_, :, h, pl.ds((r // 2) * 2 * JL, 2 * JL), :].astype(F32)
        return tile.reshape(block // JL, 2, JL, LANES)[:, r % 2].reshape(block, LANES)

    def finish_scaled(k):
        lanes = pl.ds(k * WIDE, WIDE)
        for r in range(ROWS):
            @pl.loop(0, NZ)
            def _(z_):
                rows = pl.ds(z_ * block, block)
                for h in range(NC):
                    gs = unpack(k, r, z_, h)
                    tw_acc[r, rows, :] += gs * inner[r, rows, pl.ds(k * WIDE + h * LANES, LANES)]
                    gia[rows, pl.ds(h * LANES, LANES)] = (gs * tw_cols[r, rows, :]).astype(BF)

            add_term(1, gia[...], acts[r, :, lanes])
            inner[r, :, lanes] = jnp.dot(f_t[...], gia[...], preferred_element_type=F32)

    def finish_block(k, z_):
        rows = pl.ds(z_ * block, block)
        for r in range(ROWS):
            for h in range(NC):
                lanes = pl.ds(k * WIDE + h * LANES, LANES)
                gate = go[r, rows, lanes].astype(F32) * unpack(CHUNKS + k, r, z_, h)
                gi[r, rows, lanes] = (gate + inner[r, rows, lanes]).astype(BF)

    def finish_mixed(k):
        @pl.loop(0, NZ)
        def _(z_):
            finish_block(k, z_)

    def finish_last():
        k = CHUNKS - 1

        @pl.loop(0, NZ)
        def _(i):
            z_ = jnp.where(i == 0, z, nth(jnp.maximum(i - 1, 0)))
            wait(rzr.at[2 * CHUNKS - 1, z_], last_recv.at[z_])
            finish_block(k, z_)

    def reduce_plane(which):
        unit = 4 * CHUNKS + which

        @pl.loop(1, plane)
        def _(d):
            y_, x_, c_, device = plane_peer(d)
            remote(
                terms.at[which, c_, y_, :, x_], rs_a.at[which, here], p_send.at[unit], p_recv.at[unit], device
            )

        local(terms.at[which, core, y, :, x], rs_a.at[which, here], p_recv.at[unit])

    def reduce_z(which):
        unit = 4 * CHUNKS + which
        wait(rs_a.at[which], p_recv.at[unit])
        total = rs_a[which, 0]
        for i in range(1, plane):
            total += rs_a[which, i]
        rs_bs[which] = total

        @pl.loop(1, NZ)
        def _(d):
            z_, device = z_peer(d)
            remote(rs_bs.at[which, z_], rs_b.at[which, z], b_send.at[which], b_recv.at[which], device)

        local(rs_bs.at[which, z], rs_b.at[which, z], b_recv.at[which])

    def reduce_last(which):
        wait(rs_b.at[which], b_recv.at[which])
        total = rs_b[which, 0]
        for i in range(1, NZ):
            total += rs_b[which, i]
        rs_cs[which] = total
        here_ = dp * NC + core

        @pl.loop(1, 2 * NC)
        def _(d):
            at = (here_ + d) % (2 * NC)
            device = {"seq": seq_of(y, z, x, at % NC), "dp": at // NC}
            remote(rs_cs.at[which], rs_c.at[which, here_], c_send.at[which], c_recv.at[which], device)

        local(rs_cs.at[which], rs_c.at[which, here_], c_recv.at[which])

    def reduced(which, out):
        wait(rs_c.at[which], c_recv.at[which])
        both = rs_c[which, :NC] + rs_c[which, NC:]
        full = jnp.concatenate([both[i] for i in range(NC)], axis=1)
        out[...] = jnp.where(core == 0, full[:ROWS], full[ROWS:])

    def send_twiddle():
        rows = [jnp.sum(tw_acc[r].T, axis=0, keepdims=True) for r in range(ROWS)]
        tw_send[...] = jnp.concatenate(rows + rows, axis=0)
        remote(tw_send, tw_recv, t_send.at[0], t_recv.at[0], {"seq": seq, "dp": 1 - dp})

    def drain():
        for unit in range(CHUNKS, 2 * CHUNKS):
            wait_z_sent(zs.at[0], unit)
        for unit in range(2 * CHUNKS, 4 * CHUNKS - 1):
            wait_z_sent(rzs.at[0], unit)
        for unit in range(4 * CHUNKS):
            if not 2 * CHUNKS <= unit < 3 * CHUNKS:
                wait_plane_sent(unit)
        for which in range(2):
            wait(rs_a.at[which, pl.ds(0, plane - 1)], p_send.at[4 * CHUNKS + which])
            wait(rs_b.at[which, pl.ds(0, NZ - 1)], b_send.at[which])
            wait(rs_c.at[which, pl.ds(0, 2 * NC - 1)], c_send.at[which])
        wait(tw_recv, t_send.at[0])

    pl.semaphore_wait(barrier, NZ - 1 + plane - 1 + NC)
    send_first()
    make_gm(1)
    send_out(1)
    make_gm(2)
    prepare()
    for tick in range(4 * CHUNKS):
        out = tick < 2 * CHUNKS
        if out:
            wait_z(zr.at[tick], tick)
        elif tick < 4 * CHUNKS - 1:
            wait_z(rzr.at[tick - 2 * CHUNKS], tick)
        if tick == 2 * CHUNKS + 1:
            reduce_z(0)
        if tick == 3 * CHUNKS:
            reduce_z(1)
        after = tick + 2
        if after < 2 * CHUNKS:
            send_out(after)
        elif after < 4 * CHUNKS:
            wait(rzs.at[after - 2 * CHUNKS], p_recv.at[after])
            if after < 4 * CHUNKS - 1:
                send_back(after - 2 * CHUNKS)
            else:
                send_last()
        if out:
            send_plane_out(tick)
        if tick < CHUNKS:
            wait_z_sent(zs.at[tick % CHUNKS], tick)
            make_scaled(tick)
        if 1 <= tick <= 2 * CHUNKS:
            u = tick - 1
            wait(pr.at[u], p_recv.at[u])
            if u >= CHUNKS:
                wait_plane_sent(2 * CHUNKS + u - CHUNKS)
            mix(u)
            send_plane_back(u)
        if tick == 2 * CHUNKS:
            reduce_plane(0)
        if tick == 2 * CHUNKS + 2:
            reduce_last(0)
        if 2 * CHUNKS <= tick < 3 * CHUNKS:
            finish_scaled(tick - 2 * CHUNKS)
        if tick == 3 * CHUNKS - 1:
            reduce_plane(1)
            send_twiddle()
        if tick == 3 * CHUNKS:
            reduced(0, g_outer)
        if tick == 3 * CHUNKS + 1:
            reduce_last(1)
        if 3 * CHUNKS <= tick < 4 * CHUNKS - 1:
            finish_mixed(tick - 3 * CHUNKS)

    reduced(1, g_inner)
    wait(tw_recv, t_recv.at[0])
    g_tw[...] = tw_send[:ROWS] + tw_recv[:ROWS]

    drain()
    finish_last()
    wait_z_sent(rzs.at[0], 4 * CHUNKS - 1)


def hand_over(*refs):
    sems = refs[-1]
    pairs = [(refs[0].at[r], refs[4].at[r]) for r in range(ROWS)]
    pairs += list(zip(refs[1:4], refs[5:8]))
    copies = [pltpu.make_async_copy(src, dst, sems.at[i]) for i, (src, dst) in enumerate(pairs)]
    for copy in copies:
        copy.start()
    for copy in copies:
        copy.wait()


def per_device(activations, grad_output, outer_factor, inner_factor, twiddle):
    acts, grads = activations[0], grad_output[0]
    rows, n, channels = acts.shape
    assert rows == ROWS and n == JL * NY * NZ * NX and channels == CHUNKS * WIDE
    plane, block = NY * NX * NC, ROWS * JL
    dma = pltpu.SemaphoreType.DMA
    vm = pltpu.VMEM
    units = 2 * CHUNKS
    rowed = (NZ, NY * NX, NC, block, LANES)
    columned = (NY, NZ, NX * NC, block, LANES)
    part = (n // (NY * NZ * NX), n // NC)
    small = jax.ShapeDtypeStruct((ROWS, n), F32)
    any_spec = pl.BlockSpec(memory_space=pl.ANY)
    vmem_spec = pl.BlockSpec(memory_space=pltpu.VMEM)
    slots = jax.ShapeDtypeStruct((units,) + rowed, BF)
    scratch = [
        vm((ROWS, n, channels), BF),
        vm((ROWS, n, channels), BF),
        vm((n, n), BF), vm((n, n), BF), vm((n, n), BF), vm((n, n), BF),
        vm((ROWS, n), F32),
        vm((ROWS, n, LANES), F32),
        vm((ROWS, n, LANES), F32),
        vm((ROWS, n, channels), F32),
        vm((CHUNKS,) + rowed, BF),
        vm((units,) + columned, BF),
        vm((CHUNKS,) + columned, BF),
        vm((units,) + rowed, BF),
        vm((n * JL, LANES), F32),
        vm((n * JL, LANES), F32),
        vm((CHUNKS, JL // 2, n, WIDE), BF),
        vm((n, WIDE), BF),
        vm((2, NC, NY, NZ, NX) + part, F32),
        vm((2, plane, NZ) + part, F32),
        vm((2, NZ) + part, F32),
        vm((2, NZ) + part, F32),
        vm((2,) + part, F32),
        vm((2, 2 * NC) + part, F32),
        vm((2 * ROWS, n), F32),
        vm((2 * ROWS, n), F32),
        dma((2 * CHUNKS + 3,)), dma((2, NZ)), dma((NZ,)),
        dma((2 * units,)), dma((2 * units,)),
        dma((2 * units + 2,)), dma((2 * units + 2,)),
        dma((2,)), dma((2,)), dma((2,)), dma((2,)), dma((1,)), dma((1,)),
    ]
    outs = pl.pallas_call(
        kernel,
        out_shape=[pltpu.VMEM(acts.shape, BF)] + [pltpu.VMEM(small.shape, F32)] * 3 + [slots, slots],
        in_specs=[any_spec] * 5,
        out_specs=[vmem_spec, vmem_spec, vmem_spec, vmem_spec, any_spec, any_spec],
        scratch_shapes=scratch,
        compiler_params=pltpu.CompilerParams(
            collective_id=0, has_side_effects=True, vmem_limit_bytes=52 * 2**20
        ),
        name="monarch_backward",
    )(acts, grads, outer_factor, inner_factor, twiddle)
    outs = pl.pallas_call(
        hand_over,
        out_shape=[jax.ShapeDtypeStruct(o.shape, o.dtype) for o in outs[:4]],
        in_specs=[any_spec] * 4,
        out_specs=[any_spec] * 4,
        scratch_shapes=[dma((ROWS + 3,))],
        compiler_params=pltpu.CompilerParams(vmem_limit_bytes=4 * 2**20),
        name="hand_over",
    )(*outs[:4])
    return outs[0][None], outs[1], outs[2], outs[3]


def solution(mesh):
    placed = (P("dp", "seq", None, None), P("dp", "seq", None, None), P(), P(), P("seq", None))
    return jax.shard_map(
        per_device,
        mesh=mesh,
        in_specs=placed,
        out_specs=(P("dp", "seq", None, None), P("seq", None), P("seq", None), P("seq", None)),
        check_vma=False,
    )
```

```python
import functools

import jax
import jax.numpy as jnp
from jax import lax
from jax.experimental import pallas as pl
from jax.experimental.pallas import tpu as pltpu
from jax.sharding import PartitionSpec as P

NY, NZ, NX, NC = 2, 8, 4, 2
ROWS = 4
NDP = 2
QUARTERS = NDP * NC
JL = 8
CHUNKS = 3
LANES = 128
WIDE = NC * LANES
MESH = pl.DeviceIdType.MESH
BF = jnp.bfloat16
F32 = jnp.float32


def kernel(
    acts_hbm, go_hbm, outer_hbm, inner_hbm, tw_hbm,
    gi, g_outer, g_inner, g_tw, zr, rzs,
    acts, go, o_mat, f_mat, o_t, f_t, tw_rows, tw_cols, tw_acc, inner,
    zs, pr, ps, rzr, t1, t2, gm, gia, terms,
    rs_a, rs_bs, rs_b, rs_cs, rs_c, tw_send, tw_recv,
    load_sem, first_sem, last_recv, z_send, z_recv, p_send, p_recv, b_send, b_recv, c_send, c_recv, t_send, t_recv,
):
    n = o_mat.shape[0]
    block = n // NZ
    seq = lax.axis_index("seq")
    dp = lax.axis_index("dp")
    div, rem = lax.div, lax.rem
    y, z, x, core = div(seq, NZ * NX * NC), rem(div(seq, NX * NC), NZ), rem(div(seq, NC), NX), rem(seq, NC)
    here = (y * NX + x) * NC + core
    plane = NY * NX * NC

    def seq_of(y_, z_, x_, c_):
        return ((y_ * NZ + z_) * NX + x_) * NC + c_

    def in_plane(at):
        return div(at, NX * NC), rem(div(at, NC), NX), rem(at, NC)

    def z_peer(d):
        z_ = rem(z + d, NZ)
        return z_, {"seq": seq_of(y, z_, x, core)}

    def plane_peer(d):
        y_, x_, c_ = in_plane(rem(here + d, plane))
        return y_, x_, c_, {"seq": seq_of(y_, z, x_, c_)}

    def remote(src, dst, send, recv, device):
        pltpu.make_async_remote_copy(
            src_ref=src, dst_ref=dst, send_sem=send, recv_sem=recv, device_id=device, device_id_type=MESH
        ).start()

    def local(src, dst, sem):
        pltpu.make_async_copy(src, dst, sem).start()

    def wait(ref, sem):
        pltpu.make_async_copy(ref, ref, sem).wait()

    def chunk_loads(k):
        lanes = pl.ds(k * WIDE, WIDE)
        return [
            pltpu.make_async_copy(acts_hbm.at[:, :, lanes], acts.at[:, :, lanes], load_sem.at[2 * k]),
            pltpu.make_async_copy(go_hbm.at[:, :, lanes], go.at[:, :, lanes], load_sem.at[2 * k + 1]),
        ]

    weight_loads = [
        pltpu.make_async_copy(inner_hbm, f_mat, load_sem.at[2 * CHUNKS]),
        pltpu.make_async_copy(tw_hbm, tw_rows, load_sem.at[2 * CHUNKS + 1]),
        pltpu.make_async_copy(outer_hbm, o_mat, load_sem.at[2 * CHUNKS + 2]),
    ]

    def nth(i):
        return rem(z + NZ + (i // 2 + 1) * (1 - 2 * (i % 2)), NZ)

    def first_loads(z_):
        part = (slice(None), pl.ds(z_ * block, block), pl.ds(0, WIDE))
        return [
            pltpu.make_async_copy(acts_hbm.at[part], acts.at[part], first_sem.at[0, z_]),
            pltpu.make_async_copy(go_hbm.at[part], go.at[part], first_sem.at[1, z_]),
        ]

    for i in range(2):
        for copy in first_loads(nth(i)):
            copy.start()

    barrier = pltpu.get_barrier_semaphore()

    def greet(device):
        pl.semaphore_signal(barrier, 1, device_id=device, device_id_type=MESH)

    for d in range(1, NZ):
        greet(z_peer(d)[1])
    for d in range(plane):
        dy, dx, dc = d // (NX * NC), d // NC % NX, d % NC
        near = seq_of(1 - y if dy else y, z, rem(x + dx, NX), 1 - core if dc else core)
        if d:
            greet({"seq": near})
        greet({"seq": near, "dp": 1 - dp})

    @pl.loop(2, NZ - 1)
    def _(i):
        for copy in first_loads(nth(i)):
            copy.start()

    for copy in first_loads(z):
        copy.start()
    for k in range(1, CHUNKS):
        for copy in chunk_loads(k):
            copy.start()
    for copy in weight_loads:
        copy.start()

    def ascending(i):
        return i + jnp.where(i >= z, 1, 0)

    def send_z(src, dst, unit):
        late = unit >= 4 * CHUNKS - 3

        @pl.loop(0, NZ - 1)
        def _(i):
            z_ = ascending(i) if late else rem(z + 1 + i, NZ)
            device = {"seq": seq_of(y, z_, x, core)}
            remote(src.at[z_], dst.at[z], z_send.at[unit], z_recv.at[unit], device)

        local(src.at[z], dst.at[z], z_recv.at[unit])

    def wait_z(dst, unit):
        wait(dst, z_recv.at[unit])

    def wait_z_sent(src, unit):
        wait(src.at[pl.ds(0, NZ - 1)], z_send.at[unit])

    def send_out(u):
        send_z(zs.at[u % CHUNKS], zr.at[u], u)

    def send_back(u):
        send_z(rzs.at[u], rzr.at[u], 2 * CHUNKS + u)

    def send_last():
        u, unit = 2 * CHUNKS - 1, 4 * CHUNKS - 1

        @pl.loop(0, NZ - 1)
        def _(i):
            z_ = ascending(i)
            device = {"seq": seq_of(y, z_, x, core)}
            remote(rzs.at[u, z_], rzr.at[u, z], z_send.at[unit], last_recv.at[z], device)

        local(rzs.at[u, z], rzr.at[u, z], last_recv.at[z])

    def send_plane_out(u):
        @pl.loop(1, plane)
        def _(d):
            y_, x_, c_, device = plane_peer(d)
            remote(
                zr.at[u, :, y_ * NX + x_, c_], pr.at[u, y, :, x * NC + core], p_send.at[u], p_recv.at[u], device
            )

        local(zr.at[u, :, y * NX + x, core], pr.at[u, y, :, x * NC + core], p_recv.at[u])

    def send_plane_back(u):
        unit = 2 * CHUNKS + u
        slot = u % CHUNKS

        @pl.loop(1, plane)
        def _(d):
            y_, x_, c_, device = plane_peer(d)
            remote(
                ps.at[slot, y_, :, x_ * NC + c_], rzs.at[u, :, y * NX + x, core],
                p_send.at[unit], p_recv.at[unit], device,
            )

        local(ps.at[slot, y, :, x * NC + core], rzs.at[u, :, y * NX + x, core], p_recv.at[unit])

    def wait_plane_sent(unit):
        wait(t_blocks(), p_send.at[unit])

    def t_blocks():
        return pr.at[0].reshape(n // ROWS, ROWS * JL, LANES).at[pl.ds(0, (plane - 1) * NZ)]

    def pack(slot, z_, value):
        for h in range(NC):
            for pair in range(ROWS // 2):
                halves = [value(2 * pair + i, z_, h).reshape(block // JL, 1, JL, LANES) for i in range(2)]
                both = jnp.concatenate(halves, axis=1).reshape(block // JL, 2 * JL, LANES)
                zs[slot, z_, :, h, pl.ds(pair * 2 * JL, 2 * JL), :] = both.astype(BF)

    def gm_value(k):
        def value(r, z_, h):
            rows, lanes = pl.ds(z_ * block, block), pl.ds(k * WIDE + h * LANES, LANES)
            return go[r, rows, lanes].astype(F32) * acts[r, rows, lanes].astype(F32)

        return value

    def make_gm(k):
        for copy in chunk_loads(k):
            copy.wait()

        @pl.loop(0, NZ)
        def _(z_):
            pack(k, z_, gm_value(k))

    def send_first():
        @pl.loop(0, NZ - 1)
        def _(i):
            z_ = nth(i)
            for copy in first_loads(z_):
                copy.wait()
            pack(0, z_, gm_value(0))
            remote(zs.at[0, z_], zr.at[0, z], z_send.at[0], z_recv.at[0], {"seq": seq_of(y, z_, x, core)})

        for copy in first_loads(z):
            copy.wait()
        pack(0, z, gm_value(0))
        local(zs.at[0, z], zr.at[0, z], z_recv.at[0])

    def make_scaled(k):
        lanes = pl.ds(k * WIDE, WIDE)

        @pl.loop(0, ROWS)
        def _(r):
            inner[r, :, lanes] = jnp.dot(f_mat[...], acts[r, :, lanes], preferred_element_type=F32)

        def value(r, z_, h):
            rows = pl.ds(z_ * block, block)
            return inner[r, rows, pl.ds(k * WIDE + h * LANES, LANES)] * tw_cols[r, rows, :]

        @pl.loop(0, NZ)
        def _(z_):
            pack(k, z_, value)

    def prepare():
        for copy in weight_loads:
            copy.wait()
        f_t[...] = f_mat[...].astype(F32).T.astype(BF)
        o_t[...] = o_mat[...].astype(F32).T.astype(BF)
        for r in range(ROWS):
            tw_cols[r] = jnp.broadcast_to(tw_rows[r : r + 1, :], (LANES, n)).T
        tw_acc[...] = jnp.zeros_like(tw_acc)
        terms[...] = jnp.zeros_like(terms)

    def add_term(which, left, right):
        total = lax.dot_general(left, right, (((1,), (1,)), ((), ())), preferred_element_type=F32)
        lanes = n // QUARTERS
        for q in range(QUARTERS):
            part = total[:, q * lanes : (q + 1) * lanes]
            terms[which, q] += part.reshape(NY, NZ, NX, n // (NY * NZ * NX), lanes)

    def mix(u):
        k, slot = u % CHUNKS, u % CHUNKS
        rows = NX * NC * ROWS * JL

        for y_ in range(NY):
            @pl.loop(0, NZ)
            def _(z_):
                at = pl.multiple_of((y_ * NZ + z_) * rows, rows)
                t1[pl.ds(at, rows), :] = pr[u, y_, z_].astype(F32).reshape(rows, LANES)

        for q in range(JL // 2):
            two = [t1[pl.ds(2 * q + i, n, stride=JL), :] for i in range(2)]
            piece = jnp.concatenate(two, axis=1).astype(BF)
            if u < CHUNKS:
                gm[k, q] = piece
                mixed = jnp.dot(o_t[...], piece, preferred_element_type=F32)
            else:
                mixed = jnp.dot(o_mat[...], piece, preferred_element_type=F32)
                add_term(0, gm[k, q], piece)
            for i in range(2):
                t2[pl.ds(2 * q + i, n, stride=JL), :] = mixed[:, i * LANES : (i + 1) * LANES]

        for y_ in range(NY):
            @pl.loop(0, NZ)
            def _(z_):
                at = pl.multiple_of((y_ * NZ + z_) * rows, rows)
                ps[slot, y_, z_] = t2[pl.ds(at, rows), :].reshape(NX * NC, ROWS * JL, LANES).astype(BF)

    def unpack(u, r, z_, h):
        tile = rzr[u, z_, :, h, pl.ds((r // 2) * 2 * JL, 2 * JL), :].astype(F32)
        return tile.reshape(block // JL, 2, JL, LANES)[:, r % 2].reshape(block, LANES)

    def finish_scaled(k):
        lanes = pl.ds(k * WIDE, WIDE)
        for r in range(ROWS):
            @pl.loop(0, NZ)
            def _(z_):
                rows = pl.ds(z_ * block, block)
                for h in range(NC):
                    gs = unpack(k, r, z_, h)
                    tw_acc[r, rows, :] += gs * inner[r, rows, pl.ds(k * WIDE + h * LANES, LANES)]
                    gia[rows, pl.ds(h * LANES, LANES)] = (gs * tw_cols[r, rows, :]).astype(BF)

            add_term(1, gia[...], acts[r, :, lanes])
            inner[r, :, lanes] = jnp.dot(f_t[...], gia[...], preferred_element_type=F32)

    def finish_block(k, z_):
        rows = pl.ds(z_ * block, block)
        for r in range(ROWS):
            for h in range(NC):
                lanes = pl.ds(k * WIDE + h * LANES, LANES)
                gate = go[r, rows, lanes].astype(F32) * unpack(CHUNKS + k, r, z_, h)
                gi[r, rows, lanes] = (gate + inner[r, rows, lanes]).astype(BF)

    def finish_mixed(k):
        @pl.loop(0, NZ)
        def _(z_):
            finish_block(k, z_)

    def finish_last():
        k = CHUNKS - 1

        @pl.loop(0, NZ)
        def _(i):
            z_ = jnp.where(i == 0, z, nth(jnp.maximum(i - 1, 0)))
            wait(rzr.at[2 * CHUNKS - 1, z_], last_recv.at[z_])
            finish_block(k, z_)

    def reduce_plane(which):
        unit = 4 * CHUNKS + which
        own = dp * plane + here

        @pl.loop(1, NDP * plane)
        def _(d):
            at = rem(own + d, NDP * plane)
            dp_ = div(at, plane)
            y_, x_, c_ = in_plane(rem(at, plane))
            device = {"seq": seq_of(y_, z, x_, c_), "dp": dp_}
            remote(
                terms.at[which, dp_ * NC + c_, y_, :, x_], rs_a.at[which, own], p_send.at[unit], p_recv.at[unit], device
            )

        local(terms.at[which, dp * NC + core, y, :, x], rs_a.at[which, own], p_recv.at[unit])

    def reduce_z(which):
        unit = 4 * CHUNKS + which
        wait(rs_a.at[which], p_recv.at[unit])
        total = rs_a[which, 0]
        for i in range(1, NDP * plane):
            total += rs_a[which, i]
        rs_bs[which] = total

        @pl.loop(1, NZ)
        def _(d):
            z_, device = z_peer(d)
            remote(rs_bs.at[which, z_], rs_b.at[which, z], b_send.at[which], b_recv.at[which], device)

        local(rs_bs.at[which, z], rs_b.at[which, z], b_recv.at[which])

    def reduce_last(which):
        wait(rs_b.at[which], b_recv.at[which])
        total = rs_b[which, 0]
        for i in range(1, NZ):
            total += rs_b[which, i]
        rs_cs[which] = total
        here_ = dp * NC + core

        @pl.loop(1, QUARTERS)
        def _(d):
            at = rem(here_ + d, QUARTERS)
            device = {"seq": seq_of(y, z, x, rem(at, NC)), "dp": div(at, NC)}
            remote(rs_cs.at[which], rs_c.at[which, here_], c_send.at[which], c_recv.at[which], device)

        local(rs_cs.at[which], rs_c.at[which, here_], c_recv.at[which])

    def reduced(which, out):
        wait(rs_c.at[which], c_recv.at[which])
        full = jnp.concatenate([rs_c[which, q] for q in range(QUARTERS)], axis=1)
        out[...] = jnp.where(core == 0, full[:ROWS], full[ROWS:])

    def send_twiddle():
        rows = [jnp.sum(tw_acc[r].T, axis=0, keepdims=True) for r in range(ROWS)]
        tw_send[...] = jnp.concatenate(rows + rows, axis=0)
        remote(tw_send, tw_recv, t_send.at[0], t_recv.at[0], {"seq": seq, "dp": 1 - dp})

    def drain():
        for unit in range(CHUNKS, 2 * CHUNKS):
            wait_z_sent(zs.at[0], unit)
        for unit in range(2 * CHUNKS, 4 * CHUNKS - 1):
            wait_z_sent(rzs.at[0], unit)
        for unit in range(4 * CHUNKS):
            if not 2 * CHUNKS <= unit < 3 * CHUNKS:
                wait_plane_sent(unit)
        for which in range(2):
            wait(rs_a.at[which, pl.ds(0, NDP * plane - 1)], p_send.at[4 * CHUNKS + which])
            wait(rs_b.at[which, pl.ds(0, NZ - 1)], b_send.at[which])
            wait(rs_c.at[which, pl.ds(0, QUARTERS - 1)], c_send.at[which])
        wait(tw_recv, t_send.at[0])

    pl.semaphore_wait(barrier, NZ - 1 + plane - 1 + plane)
    send_first()
    make_gm(1)
    send_out(1)
    make_gm(2)
    prepare()
    for tick in range(4 * CHUNKS):
        out = tick < 2 * CHUNKS
        if out:
            wait_z(zr.at[tick], tick)
        elif tick < 4 * CHUNKS - 1:
            wait_z(rzr.at[tick - 2 * CHUNKS], tick)
        if tick == 2 * CHUNKS + 1:
            reduce_z(0)
        if tick == 3 * CHUNKS:
            reduce_z(1)
        after = tick + 2
        if after < 2 * CHUNKS:
            send_out(after)
        elif after < 4 * CHUNKS:
            wait(rzs.at[after - 2 * CHUNKS], p_recv.at[after])
            if after < 4 * CHUNKS - 1:
                send_back(after - 2 * CHUNKS)
            else:
                send_last()
        if out:
            send_plane_out(tick)
        if tick < CHUNKS:
            wait_z_sent(zs.at[tick % CHUNKS], tick)
            make_scaled(tick)
        if 1 <= tick <= 2 * CHUNKS:
            u = tick - 1
            wait(pr.at[u], p_recv.at[u])
            if u >= CHUNKS:
                wait_plane_sent(2 * CHUNKS + u - CHUNKS)
            mix(u)
            send_plane_back(u)
        if tick == 2 * CHUNKS:
            reduce_plane(0)
        if tick == 2 * CHUNKS + 2:
            reduce_last(0)
        if 2 * CHUNKS <= tick < 3 * CHUNKS:
            finish_scaled(tick - 2 * CHUNKS)
        if tick == 3 * CHUNKS - 1:
            reduce_plane(1)
            send_twiddle()
        if tick == 3 * CHUNKS:
            reduced(0, g_outer)
        if tick == 3 * CHUNKS + 1:
            reduce_last(1)
        if 3 * CHUNKS <= tick < 4 * CHUNKS - 1:
            finish_mixed(tick - 3 * CHUNKS)

    reduced(1, g_inner)
    wait(tw_recv, t_recv.at[0])
    g_tw[...] = tw_send[:ROWS] + tw_recv[:ROWS]

    drain()
    finish_last()
    wait_z_sent(rzs.at[0], 4 * CHUNKS - 1)


def hand_over(*refs):
    sems = refs[-1]
    pairs = [(refs[0].at[r], refs[4].at[r]) for r in range(ROWS)]
    pairs += list(zip(refs[1:4], refs[5:8]))
    copies = [pltpu.make_async_copy(src, dst, sems.at[i]) for i, (src, dst) in enumerate(pairs)]
    for copy in copies:
        copy.start()
    for copy in copies:
        copy.wait()


def per_device(activations, grad_output, outer_factor, inner_factor, twiddle):
    acts, grads = activations[0], grad_output[0]
    rows, n, channels = acts.shape
    assert rows == ROWS and n == JL * NY * NZ * NX and channels == CHUNKS * WIDE
    plane, block = NY * NX * NC, ROWS * JL
    dma = pltpu.SemaphoreType.DMA
    vm = pltpu.VMEM
    units = 2 * CHUNKS
    rowed = (NZ, NY * NX, NC, block, LANES)
    columned = (NY, NZ, NX * NC, block, LANES)
    part = (n // (NY * NZ * NX), n // QUARTERS)
    small = jax.ShapeDtypeStruct((ROWS, n), F32)
    any_spec = pl.BlockSpec(memory_space=pl.ANY)
    vmem_spec = pl.BlockSpec(memory_space=pltpu.VMEM)
    slots = jax.ShapeDtypeStruct((units,) + rowed, BF)
    scratch = [
        vm((ROWS, n, channels), BF),
        vm((ROWS, n, channels), BF),
        vm((n, n), BF), vm((n, n), BF), vm((n, n), BF), vm((n, n), BF),
        vm((ROWS, n), F32),
        vm((ROWS, n, LANES), F32),
        vm((ROWS, n, LANES), F32),
        vm((ROWS, n, channels), F32),
        vm((CHUNKS,) + rowed, BF),
        vm((units,) + columned, BF),
        vm((CHUNKS,) + columned, BF),
        vm((units,) + rowed, BF),
        vm((n * JL, LANES), F32),
        vm((n * JL, LANES), F32),
        vm((CHUNKS, JL // 2, n, WIDE), BF),
        vm((n, WIDE), BF),
        vm((2, QUARTERS, NY, NZ, NX) + part, F32),
        vm((2, NDP * plane, NZ) + part, F32),
        vm((2, NZ) + part, F32),
        vm((2, NZ) + part, F32),
        vm((2,) + part, F32),
        vm((2, QUARTERS) + part, F32),
        vm((2 * ROWS, n), F32),
        vm((2 * ROWS, n), F32),
        dma((2 * CHUNKS + 3,)), dma((2, NZ)), dma((NZ,)),
        dma((2 * units,)), dma((2 * units,)),
        dma((2 * units + 2,)), dma((2 * units + 2,)),
        dma((2,)), dma((2,)), dma((2,)), dma((2,)), dma((1,)), dma((1,)),
    ]
    outs = pl.pallas_call(
        kernel,
        out_shape=[pltpu.VMEM(acts.shape, BF)] + [pltpu.VMEM(small.shape, F32)] * 3 + [slots, slots],
        in_specs=[any_spec] * 5,
        out_specs=[vmem_spec, vmem_spec, vmem_spec, vmem_spec, any_spec, any_spec],
        scratch_shapes=scratch,
        compiler_params=pltpu.CompilerParams(
            collective_id=0, has_side_effects=True, vmem_limit_bytes=52 * 2**20
        ),
        name="monarch_backward",
    )(acts, grads, outer_factor, inner_factor, twiddle)
    outs = pl.pallas_call(
        hand_over,
        out_shape=[jax.ShapeDtypeStruct(o.shape, o.dtype) for o in outs[:4]],
        in_specs=[any_spec] * 4,
        out_specs=[any_spec] * 4,
        scratch_shapes=[dma((ROWS + 3,))],
        compiler_params=pltpu.CompilerParams(vmem_limit_bytes=4 * 2**20),
        name="hand_over",
    )(*outs[:4])
    return outs[0][None], outs[1], outs[2], outs[3]


def solution(mesh):
    placed = (P("dp", "seq", None, None), P("dp", "seq", None, None), P(), P(), P("seq", None))
    return jax.shard_map(
        per_device,
        mesh=mesh,
        in_specs=placed,
        out_specs=(P("dp", "seq", None, None), P("seq", None), P("seq", None), P("seq", None)),
        check_vma=False,
    )
```

```python
import functools

import jax
import jax.numpy as jnp
from jax import lax
from jax.experimental import pallas as pl
from jax.experimental.pallas import tpu as pltpu
from jax.sharding import PartitionSpec as P

NY, NZ, NX, NC = 2, 8, 4, 2
ROWS = 4
NDP = 2
QUARTERS = NDP * NC
JL = 8
CHUNKS = 3
LANES = 128
WIDE = NC * LANES
MESH = pl.DeviceIdType.MESH
BF = jnp.bfloat16
F32 = jnp.float32


def kernel(
    acts_hbm, go_hbm, outer_hbm, inner_hbm, tw_hbm,
    gi, g_outer, g_inner, g_tw, zr, rzs,
    acts, go, o_mat, f_mat, o_t, f_t, tw_rows, tw_cols, tw_acc, inner,
    zs, pr, ps, rzr, t1, t2, gm, gia, terms,
    rs_a, rs_bs, rs_b, rs_cs, rs_c, tw_send, tw_recv,
    load_sem, first_sem, last_recv, z_send, z_recv, p_send, p_recv, b_send, b_recv, c_send, c_recv, t_send, t_recv,
):
    n = o_mat.shape[0]
    block = n // NZ
    seq = lax.axis_index("seq")
    dp = lax.axis_index("dp")
    div, rem = lax.div, lax.rem
    y, z, x, core = div(seq, NZ * NX * NC), rem(div(seq, NX * NC), NZ), rem(div(seq, NC), NX), rem(seq, NC)
    here = (y * NX + x) * NC + core
    plane = NY * NX * NC

    def seq_of(y_, z_, x_, c_):
        return ((y_ * NZ + z_) * NX + x_) * NC + c_

    def in_plane(at):
        return div(at, NX * NC), rem(div(at, NC), NX), rem(at, NC)

    def z_peer(d):
        z_ = rem(z + d, NZ)
        return z_, {"seq": seq_of(y, z_, x, core)}

    def plane_peer(d):
        y_, x_, c_ = in_plane(rem(here + d, plane))
        return y_, x_, c_, {"seq": seq_of(y_, z, x_, c_)}

    def remote(src, dst, send, recv, device):
        pltpu.make_async_remote_copy(
            src_ref=src, dst_ref=dst, send_sem=send, recv_sem=recv, device_id=device, device_id_type=MESH
        ).start()

    def local(src, dst, sem):
        pltpu.make_async_copy(src, dst, sem).start()

    def wait(ref, sem):
        pltpu.make_async_copy(ref, ref, sem).wait()

    def chunk_loads(k):
        lanes = pl.ds(k * WIDE, WIDE)
        return [
            pltpu.make_async_copy(acts_hbm.at[:, :, lanes], acts.at[:, :, lanes], load_sem.at[2 * k]),
            pltpu.make_async_copy(go_hbm.at[:, :, lanes], go.at[:, :, lanes], load_sem.at[2 * k + 1]),
        ]

    weight_loads = [
        pltpu.make_async_copy(inner_hbm, f_mat, load_sem.at[2 * CHUNKS]),
        pltpu.make_async_copy(tw_hbm, tw_rows, load_sem.at[2 * CHUNKS + 1]),
        pltpu.make_async_copy(outer_hbm, o_mat, load_sem.at[2 * CHUNKS + 2]),
    ]

    def nth(i):
        return rem(z + NZ + (i // 2 + 1) * (1 - 2 * (i % 2)), NZ)

    def first_loads(z_):
        part = (slice(None), pl.ds(z_ * block, block), pl.ds(0, WIDE))
        return [
            pltpu.make_async_copy(acts_hbm.at[part], acts.at[part], first_sem.at[0, z_]),
            pltpu.make_async_copy(go_hbm.at[part], go.at[part], first_sem.at[1, z_]),
        ]

    for i in range(2):
        for copy in first_loads(nth(i)):
            copy.start()

    barrier = pltpu.get_barrier_semaphore()

    def greet(device):
        pl.semaphore_signal(barrier, 1, device_id=device, device_id_type=MESH)

    for d in range(1, NZ):
        greet(z_peer(d)[1])
    for d in range(plane):
        dy, dx, dc = d // (NX * NC), d // NC % NX, d % NC
        near = seq_of(1 - y if dy else y, z, rem(x + dx, NX), 1 - core if dc else core)
        if d:
            greet({"seq": near})
        greet({"seq": near, "dp": 1 - dp})

    @pl.loop(2, NZ - 1)
    def _(i):
        for copy in first_loads(nth(i)):
            copy.start()

    for copy in first_loads(z):
        copy.start()
    for k in range(1, CHUNKS):
        for copy in chunk_loads(k):
            copy.start()
    for copy in weight_loads:
        copy.start()

    def ascending(i):
        return i + jnp.where(i >= z, 1, 0)

    def send_z(src, dst, unit):
        late = unit >= 4 * CHUNKS - 3

        @pl.loop(0, NZ - 1)
        def _(i):
            z_ = ascending(i) if late else rem(z + 1 + i, NZ)
            device = {"seq": seq_of(y, z_, x, core)}
            remote(src.at[z_], dst.at[z], z_send.at[unit], z_recv.at[unit], device)

        local(src.at[z], dst.at[z], z_recv.at[unit])

    def wait_z(dst, unit):
        wait(dst, z_recv.at[unit])

    def wait_z_sent(src, unit):
        wait(src.at[pl.ds(0, NZ - 1)], z_send.at[unit])

    def send_out(u):
        send_z(zs.at[u % CHUNKS], zr.at[u], u)

    def send_back(u):
        send_z(rzs.at[u], rzr.at[u], 2 * CHUNKS + u)

    def send_last():
        u, unit = 2 * CHUNKS - 1, 4 * CHUNKS - 1

        @pl.loop(0, NZ - 1)
        def _(i):
            z_ = ascending(i)
            device = {"seq": seq_of(y, z_, x, core)}
            remote(rzs.at[u, z_], rzr.at[u, z], z_send.at[unit], last_recv.at[z], device)

        local(rzs.at[u, z], rzr.at[u, z], last_recv.at[z])

    def send_plane_out(u):
        @pl.loop(1, plane)
        def _(d):
            y_, x_, c_, device = plane_peer(d)
            remote(
                zr.at[u, :, y_ * NX + x_, c_], pr.at[u, y, :, x * NC + core], p_send.at[u], p_recv.at[u], device
            )

        local(zr.at[u, :, y * NX + x, core], pr.at[u, y, :, x * NC + core], p_recv.at[u])

    def send_plane_back(u):
        unit = 2 * CHUNKS + u
        slot = u % CHUNKS

        @pl.loop(1, plane)
        def _(d):
            y_, x_, c_, device = plane_peer(d)
            remote(
                ps.at[slot, y_, :, x_ * NC + c_], rzs.at[u, :, y * NX + x, core],
                p_send.at[unit], p_recv.at[unit], device,
            )

        local(ps.at[slot, y, :, x * NC + core], rzs.at[u, :, y * NX + x, core], p_recv.at[unit])

    def wait_plane_sent(unit):
        wait(t_blocks(), p_send.at[unit])

    def t_blocks():
        return pr.at[0].reshape(n // ROWS, ROWS * JL, LANES).at[pl.ds(0, (plane - 1) * NZ)]

    def pack(slot, z_, value):
        for h in range(NC):
            for pair in range(ROWS // 2):
                halves = [value(2 * pair + i, z_, h).reshape(block // JL, 1, JL, LANES) for i in range(2)]
                both = jnp.concatenate(halves, axis=1).reshape(block // JL, 2 * JL, LANES)
                zs[slot, z_, :, h, pl.ds(pair * 2 * JL, 2 * JL), :] = both.astype(BF)

    def gm_value(k):
        def value(r, z_, h):
            rows, lanes = pl.ds(z_ * block, block), pl.ds(k * WIDE + h * LANES, LANES)
            return go[r, rows, lanes].astype(F32) * acts[r, rows, lanes].astype(F32)

        return value

    def make_gm(k):
        for copy in chunk_loads(k):
            copy.wait()

        @pl.loop(0, NZ)
        def _(z_):
            pack(k, z_, gm_value(k))

    def make_first(i):
        z_ = nth(i)
        for copy in first_loads(z_):
            copy.wait()
        pack(0, z_, gm_value(0))

    def send_first():
        @pl.loop(0, NZ - 1)
        def _(i):
            z_ = nth(i)

            @pl.when(i >= 2)
            def _():
                make_first(i)

            remote(zs.at[0, z_], zr.at[0, z], z_send.at[0], z_recv.at[0], {"seq": seq_of(y, z_, x, core)})

        for copy in first_loads(z):
            copy.wait()
        pack(0, z, gm_value(0))
        local(zs.at[0, z], zr.at[0, z], z_recv.at[0])

    def make_scaled(k):
        lanes = pl.ds(k * WIDE, WIDE)

        @pl.loop(0, ROWS)
        def _(r):
            inner[r, :, lanes] = jnp.dot(f_mat[...], acts[r, :, lanes], preferred_element_type=F32)

        def value(r, z_, h):
            rows = pl.ds(z_ * block, block)
            return inner[r, rows, pl.ds(k * WIDE + h * LANES, LANES)] * tw_cols[r, rows, :]

        @pl.loop(0, NZ)
        def _(z_):
            pack(k, z_, value)

    def prepare():
        for copy in weight_loads:
            copy.wait()
        f_t[...] = f_mat[...].astype(F32).T.astype(BF)
        o_t[...] = o_mat[...].astype(F32).T.astype(BF)
        for r in range(ROWS):
            tw_cols[r] = jnp.broadcast_to(tw_rows[r : r + 1, :], (LANES, n)).T
        tw_acc[...] = jnp.zeros_like(tw_acc)
        terms[...] = jnp.zeros_like(terms)

    def add_term(which, left, right):
        total = lax.dot_general(left, right, (((1,), (1,)), ((), ())), preferred_element_type=F32)
        lanes = n // QUARTERS
        for q in range(QUARTERS):
            part = total[:, q * lanes : (q + 1) * lanes]
            terms[which, q] += part.reshape(NY, NZ, NX, n // (NY * NZ * NX), lanes)

    def mix(u):
        k, slot = u % CHUNKS, u % CHUNKS
        rows = NX * NC * ROWS * JL

        for y_ in range(NY):
            @pl.loop(0, NZ)
            def _(z_):
                at = pl.multiple_of((y_ * NZ + z_) * rows, rows)
                t1[pl.ds(at, rows), :] = pr[u, y_, z_].astype(F32).reshape(rows, LANES)

        for q in range(JL // 2):
            two = [t1[pl.ds(2 * q + i, n, stride=JL), :] for i in range(2)]
            piece = jnp.concatenate(two, axis=1).astype(BF)
            if u < CHUNKS:
                gm[k, q] = piece
                mixed = jnp.dot(o_t[...], piece, preferred_element_type=F32)
            else:
                mixed = jnp.dot(o_mat[...], piece, preferred_element_type=F32)
                add_term(0, gm[k, q], piece)
            for i in range(2):
                t2[pl.ds(2 * q + i, n, stride=JL), :] = mixed[:, i * LANES : (i + 1) * LANES]

        for y_ in range(NY):
            @pl.loop(0, NZ)
            def _(z_):
                at = pl.multiple_of((y_ * NZ + z_) * rows, rows)
                ps[slot, y_, z_] = t2[pl.ds(at, rows), :].reshape(NX * NC, ROWS * JL, LANES).astype(BF)

    def unpack(u, r, z_, h):
        tile = rzr[u, z_, :, h, pl.ds((r // 2) * 2 * JL, 2 * JL), :].astype(F32)
        return tile.reshape(block // JL, 2, JL, LANES)[:, r % 2].reshape(block, LANES)

    def finish_scaled(k):
        lanes = pl.ds(k * WIDE, WIDE)
        for r in range(ROWS):
            @pl.loop(0, NZ)
            def _(z_):
                rows = pl.ds(z_ * block, block)
                for h in range(NC):
                    gs = unpack(k, r, z_, h)
                    tw_acc[r, rows, :] += gs * inner[r, rows, pl.ds(k * WIDE + h * LANES, LANES)]
                    gia[rows, pl.ds(h * LANES, LANES)] = (gs * tw_cols[r, rows, :]).astype(BF)

            add_term(1, gia[...], acts[r, :, lanes])
            inner[r, :, lanes] = jnp.dot(f_t[...], gia[...], preferred_element_type=F32)

    def finish_block(k, z_):
        rows = pl.ds(z_ * block, block)
        for r in range(ROWS):
            for h in range(NC):
                lanes = pl.ds(k * WIDE + h * LANES, LANES)
                gate = go[r, rows, lanes].astype(F32) * unpack(CHUNKS + k, r, z_, h)
                gi[r, rows, lanes] = (gate + inner[r, rows, lanes]).astype(BF)

    def finish_mixed(k):
        @pl.loop(0, NZ)
        def _(z_):
            finish_block(k, z_)

    def finish_last():
        k = CHUNKS - 1

        @pl.loop(0, NZ)
        def _(i):
            z_ = jnp.where(i == 0, z, nth(jnp.maximum(i - 1, 0)))
            wait(rzr.at[2 * CHUNKS - 1, z_], last_recv.at[z_])
            finish_block(k, z_)

    def reduce_plane(which):
        unit = 4 * CHUNKS + which
        own = dp * plane + here

        @pl.loop(1, NDP * plane)
        def _(d):
            at = rem(own + d, NDP * plane)
            dp_ = div(at, plane)
            y_, x_, c_ = in_plane(rem(at, plane))
            device = {"seq": seq_of(y_, z, x_, c_), "dp": dp_}
            remote(
                terms.at[which, dp_ * NC + c_, y_, :, x_], rs_a.at[which, own], p_send.at[unit], p_recv.at[unit], device
            )

        local(terms.at[which, dp * NC + core, y, :, x], rs_a.at[which, own], p_recv.at[unit])

    def reduce_z(which):
        unit = 4 * CHUNKS + which
        wait(rs_a.at[which], p_recv.at[unit])
        total = rs_a[which, 0]
        for i in range(1, NDP * plane):
            total += rs_a[which, i]
        rs_bs[which] = total

        @pl.loop(1, NZ)
        def _(d):
            z_, device = z_peer(d)
            remote(rs_bs.at[which, z_], rs_b.at[which, z], b_send.at[which], b_recv.at[which], device)

        local(rs_bs.at[which, z], rs_b.at[which, z], b_recv.at[which])

    def reduce_last(which):
        wait(rs_b.at[which], b_recv.at[which])
        total = rs_b[which, 0]
        for i in range(1, NZ):
            total += rs_b[which, i]
        rs_cs[which] = total
        here_ = dp * NC + core

        @pl.loop(1, QUARTERS)
        def _(d):
            at = rem(here_ + d, QUARTERS)
            device = {"seq": seq_of(y, z, x, rem(at, NC)), "dp": div(at, NC)}
            remote(rs_cs.at[which], rs_c.at[which, here_], c_send.at[which], c_recv.at[which], device)

        local(rs_cs.at[which], rs_c.at[which, here_], c_recv.at[which])

    def reduced(which, out):
        wait(rs_c.at[which], c_recv.at[which])
        full = jnp.concatenate([rs_c[which, q] for q in range(QUARTERS)], axis=1)
        out[...] = jnp.where(core == 0, full[:ROWS], full[ROWS:])

    def send_twiddle():
        rows = [jnp.sum(tw_acc[r].T, axis=0, keepdims=True) for r in range(ROWS)]
        tw_send[...] = jnp.concatenate(rows + rows, axis=0)
        remote(tw_send, tw_recv, t_send.at[0], t_recv.at[0], {"seq": seq, "dp": 1 - dp})

    def drain():
        for unit in range(CHUNKS, 2 * CHUNKS):
            wait_z_sent(zs.at[0], unit)
        for unit in range(2 * CHUNKS, 4 * CHUNKS - 1):
            wait_z_sent(rzs.at[0], unit)
        for unit in range(4 * CHUNKS):
            if not 2 * CHUNKS <= unit < 3 * CHUNKS:
                wait_plane_sent(unit)
        for which in range(2):
            wait(rs_a.at[which, pl.ds(0, NDP * plane - 1)], p_send.at[4 * CHUNKS + which])
            wait(rs_b.at[which, pl.ds(0, NZ - 1)], b_send.at[which])
            wait(rs_c.at[which, pl.ds(0, QUARTERS - 1)], c_send.at[which])
        wait(tw_recv, t_send.at[0])

    @pl.loop(0, 2)
    def _(i):
        make_first(i)

    pl.semaphore_wait(barrier, NZ - 1 + plane - 1 + plane)
    send_first()
    make_gm(1)
    send_out(1)
    make_gm(2)
    prepare()
    for tick in range(4 * CHUNKS):
        out = tick < 2 * CHUNKS
        if out:
            wait_z(zr.at[tick], tick)
        elif tick < 4 * CHUNKS - 1:
            wait_z(rzr.at[tick - 2 * CHUNKS], tick)
        if tick == 2 * CHUNKS + 1:
            reduce_z(0)
        if tick == 3 * CHUNKS:
            reduce_z(1)
        after = tick + 2
        if after < 2 * CHUNKS:
            send_out(after)
        elif after < 4 * CHUNKS:
            wait(rzs.at[after - 2 * CHUNKS], p_recv.at[after])
            if after < 4 * CHUNKS - 1:
                send_back(after - 2 * CHUNKS)
            else:
                send_last()
        if out:
            send_plane_out(tick)
        if tick < CHUNKS:
            wait_z_sent(zs.at[tick % CHUNKS], tick)
            make_scaled(tick)
        if 1 <= tick <= 2 * CHUNKS:
            u = tick - 1
            wait(pr.at[u], p_recv.at[u])
            if u >= CHUNKS:
                wait_plane_sent(2 * CHUNKS + u - CHUNKS)
            mix(u)
            send_plane_back(u)
        if tick == 2 * CHUNKS:
            reduce_plane(0)
        if tick == 2 * CHUNKS + 2:
            reduce_last(0)
        if 2 * CHUNKS <= tick < 3 * CHUNKS:
            finish_scaled(tick - 2 * CHUNKS)
        if tick == 3 * CHUNKS - 1:
            reduce_plane(1)
            send_twiddle()
        if tick == 3 * CHUNKS:
            reduced(0, g_outer)
        if tick == 3 * CHUNKS + 1:
            reduce_last(1)
        if 3 * CHUNKS <= tick < 4 * CHUNKS - 1:
            finish_mixed(tick - 3 * CHUNKS)

    reduced(1, g_inner)
    wait(tw_recv, t_recv.at[0])
    g_tw[...] = tw_send[:ROWS] + tw_recv[:ROWS]

    drain()
    finish_last()
    wait_z_sent(rzs.at[0], 4 * CHUNKS - 1)


def hand_over(*refs):
    sems = refs[-1]
    pairs = [(refs[0].at[r], refs[4].at[r]) for r in range(ROWS)]
    pairs += list(zip(refs[1:4], refs[5:8]))
    copies = [pltpu.make_async_copy(src, dst, sems.at[i]) for i, (src, dst) in enumerate(pairs)]
    for copy in copies:
        copy.start()
    for copy in copies:
        copy.wait()


def per_device(activations, grad_output, outer_factor, inner_factor, twiddle):
    acts, grads = activations[0], grad_output[0]
    rows, n, channels = acts.shape
    assert rows == ROWS and n == JL * NY * NZ * NX and channels == CHUNKS * WIDE
    plane, block = NY * NX * NC, ROWS * JL
    dma = pltpu.SemaphoreType.DMA
    vm = pltpu.VMEM
    units = 2 * CHUNKS
    rowed = (NZ, NY * NX, NC, block, LANES)
    columned = (NY, NZ, NX * NC, block, LANES)
    part = (n // (NY * NZ * NX), n // QUARTERS)
    small = jax.ShapeDtypeStruct((ROWS, n), F32)
    any_spec = pl.BlockSpec(memory_space=pl.ANY)
    vmem_spec = pl.BlockSpec(memory_space=pltpu.VMEM)
    slots = jax.ShapeDtypeStruct((units,) + rowed, BF)
    scratch = [
        vm((ROWS, n, channels), BF),
        vm((ROWS, n, channels), BF),
        vm((n, n), BF), vm((n, n), BF), vm((n, n), BF), vm((n, n), BF),
        vm((ROWS, n), F32),
        vm((ROWS, n, LANES), F32),
        vm((ROWS, n, LANES), F32),
        vm((ROWS, n, channels), F32),
        vm((CHUNKS,) + rowed, BF),
        vm((units,) + columned, BF),
        vm((CHUNKS,) + columned, BF),
        vm((units,) + rowed, BF),
        vm((n * JL, LANES), F32),
        vm((n * JL, LANES), F32),
        vm((CHUNKS, JL // 2, n, WIDE), BF),
        vm((n, WIDE), BF),
        vm((2, QUARTERS, NY, NZ, NX) + part, F32),
        vm((2, NDP * plane, NZ) + part, F32),
        vm((2, NZ) + part, F32),
        vm((2, NZ) + part, F32),
        vm((2,) + part, F32),
        vm((2, QUARTERS) + part, F32),
        vm((2 * ROWS, n), F32),
        vm((2 * ROWS, n), F32),
        dma((2 * CHUNKS + 3,)), dma((2, NZ)), dma((NZ,)),
        dma((2 * units,)), dma((2 * units,)),
        dma((2 * units + 2,)), dma((2 * units + 2,)),
        dma((2,)), dma((2,)), dma((2,)), dma((2,)), dma((1,)), dma((1,)),
    ]
    outs = pl.pallas_call(
        kernel,
        out_shape=[pltpu.VMEM(acts.shape, BF)] + [pltpu.VMEM(small.shape, F32)] * 3 + [slots, slots],
        in_specs=[any_spec] * 5,
        out_specs=[vmem_spec, vmem_spec, vmem_spec, vmem_spec, any_spec, any_spec],
        scratch_shapes=scratch,
        compiler_params=pltpu.CompilerParams(
            collective_id=0, has_side_effects=True, vmem_limit_bytes=52 * 2**20
        ),
        name="monarch_backward",
    )(acts, grads, outer_factor, inner_factor, twiddle)
    outs = pl.pallas_call(
        hand_over,
        out_shape=[jax.ShapeDtypeStruct(o.shape, o.dtype) for o in outs[:4]],
        in_specs=[any_spec] * 4,
        out_specs=[any_spec] * 4,
        scratch_shapes=[dma((ROWS + 3,))],
        compiler_params=pltpu.CompilerParams(vmem_limit_bytes=4 * 2**20),
        name="hand_over",
    )(*outs[:4])
    return outs[0][None], outs[1], outs[2], outs[3]


def solution(mesh):
    placed = (P("dp", "seq", None, None), P("dp", "seq", None, None), P(), P(), P("seq", None))
    return jax.shard_map(
        per_device,
        mesh=mesh,
        in_specs=placed,
        out_specs=(P("dp", "seq", None, None), P("seq", None), P("seq", None), P("seq", None)),
        check_vma=False,
    )
```
